32 devices in a mesh: groups: 2 (over x), band: 16 (over z, y, core).
Axes of the slice: x: 2, y: 2, z: 4, core: 2. Of those that a mesh axis runs over, the one named last changes fastest.
Arguments:
- nest_tokens: bfloat16 [16384, 256], P(('groups', 'band')), parts along dimension 0
- global_tokens: bfloat16 [4096, 256], P(('groups', 'band')), parts along dimension 0
- block_ids: int32 [128, 4], P(('groups', 'band')), parts along dimension 0, may hold values from 0 to 15, as said below
- list_length: int32 [128], P(('groups', 'band')), parts along dimension 0, may hold values from 2 to 4, as said below
- w_query: bfloat16 [256, 256], replicated, may hold values from -0.375 to 0.375
- w_keyval: bfloat16 [256, 512], replicated, may hold values from -0.375 to 0.375
- w_out: bfloat16 [256, 256], replicated, may hold values from -0.375 to 0.375
- d_output: bfloat16 [16384, 256], P(('groups', 'band')), parts along dimension 0, may hold values from -6 to 6
Outputs:
- output: bfloat16 [16384, 256], P(('groups', 'band')), parts along dimension 0
- d_nest: bfloat16 [16384, 256], P(('groups', 'band')), parts along dimension 0
- d_global: bfloat16 [4096, 256], P(('groups', 'band')), parts along dimension 0
- grad_query: float32 [512, 256], P('groups'), parts along dimension 0
- grad_keyval: float32 [512, 512], P('groups'), parts along dimension 0
- grad_out: float32 [512, 256], P('groups'), parts along dimension 0
The draws below stay inside these ranges and needn't reach their ends.
There are 2 independent parts, one for each index of `groups`. The reference program is written for one: setup_inputs(seed, part) draws one part's arguments, and reference() takes and returns one part's arrays. A program takes and returns all parts, laid end to end along the dimension named above; an argument that names none is the same for every part. Nothing has to cross between parts.
Inputs may be any that keep to these rules, and one draw needn't show every extreme that they name: `block_ids`: each row holds 4 different global block numbers, all owned by the aligned group of 16 devices of band that holds the nest block; the global blocks of device d are d*1 to (d+1) - 1. Only the first list_length[b] entries of row b are used.
All inputs are finite; a program needn't handle non-finite values.
Results may differ from the reference program's by a relative error of at most 0.0095.
The reference program's roundings to bfloat16 on the way (of `queries`, `pairs`, `grad_attn`, `probs_low`, `attended`, `d_scores` and `d_queries`) count: a program that leaves them out, or rounds other values in their place, can miss the bound.
Values may be sent and summed in bfloat16 or wider, within the bound.
A program may use at most 128 MiB of HBM per device.

```python
import jax
import jax.numpy as jnp
from jax import lax

D = 256
HD = 32
BT = 128
GB = 128
LIST = 4
SUB = 16
NB_DEV = 4
BLK_DEV = 1
NBLK = 64
GBLK = 16
NEST_TOKENS = 8192
GLOB_TOKENS = 2048


def feature_rows(key, count, row_spread, bound):
    first_key, second_key = jax.random.split(key)
    values = jax.random.normal(first_key, (count, D), jnp.float32)
    row_scales = jnp.exp(jax.random.uniform(second_key, (count, 1), jnp.float32) * jnp.log(row_spread))
    return jnp.clip(values * row_scales, -bound, bound)


def draw_nest_tokens(key, part):
    key = jax.random.fold_in(key, 11)
    values = feature_rows(key, NEST_TOKENS, 1.0, 6.0)
    return values.astype(jnp.bfloat16)


def draw_global_tokens(key, part):
    key = jax.random.fold_in(key, 13)
    values = feature_rows(key, GLOB_TOKENS, 1.0, 6.0)
    return values.astype(jnp.bfloat16)


def draw_block_ids(key, part):
    key = jax.random.fold_in(key, 17)
    first_key, second_key = jax.random.split(key)
    region_size = SUB * BLK_DEV
    anchor = jax.random.randint(first_key, (NBLK,), 0, region_size, dtype=jnp.int32)
    anchor = anchor.at[0].set(0).at[NBLK - 1].set(region_size - 1)
    stride = jax.random.randint(second_key, (NBLK,), 1, 6, dtype=jnp.int32)
    slot_index = jnp.arange(LIST, dtype=jnp.int32)
    local_ids = (anchor[:, None] + slot_index[None, :] * stride[:, None]) % region_size
    holder = jnp.arange(NBLK, dtype=jnp.int32) // NB_DEV
    region_base = holder // SUB * region_size
    return (region_base[:, None] + local_ids).astype(jnp.int32)


def draw_list_length(key, part):
    key = jax.random.fold_in(key, 19)
    counts = jax.random.randint(key, (NBLK,), 2, 5, dtype=jnp.int32)
    return counts.at[0].set(4).at[1].set(2)


def steps_of(key, shape, shards, smallest, top_value):
    def one(position, blocks):
        heights = jax.random.uniform(jax.random.fold_in(jax.random.fold_in(key, 6), position), (blocks,), jnp.float32, smallest / len(shards), top_value / len(shards))
        return jnp.repeat(jnp.exp(heights), shape[position] // blocks).reshape((-1,) + (1,) * (len(shape) - position - 1))

    level = one(*shards[0])
    for cut in shards[1:]:
        level = level * one(*cut)
    return level


def centred(stream_key, shape, width, limit, pieces=(), kind=jnp.bfloat16):
    result = width * jax.random.normal(stream_key, shape, jnp.float32)
    if pieces:
        result = result * steps_of(stream_key, shape, pieces, -0.22, 0.18)
    return jnp.clip(result, -limit, limit).astype(kind)


def setup_inputs(seed: int = 0, part: int = 0) -> dict:
    key_list = jax.random.split(jax.random.key(seed), 9)
    own_keys = jax.random.split(jax.random.fold_in(key_list[8], part), 9)
    nest_tokens = draw_nest_tokens(jax.random.fold_in(jax.random.fold_in(key_list[8], part), 71), part)
    global_tokens = draw_global_tokens(jax.random.fold_in(jax.random.fold_in(key_list[8], part), 71), part)
    block_ids = draw_block_ids(jax.random.fold_in(jax.random.fold_in(key_list[8], part), 71), part)
    list_length = draw_list_length(jax.random.fold_in(jax.random.fold_in(key_list[8], part), 71), part)
    w_query = centred(key_list[4], (D, D), D ** -0.5, 0.375)
    w_keyval = centred(key_list[5], (D, 2 * D), D ** -0.5, 0.375)
    w_out = centred(key_list[6], (D, D), D ** -0.5, 0.375)
    d_output = centred(own_keys[7], (NEST_TOKENS, D), 1.0, 6.0, ((0, 16),))
    return {"nest_tokens": nest_tokens, "global_tokens": global_tokens, "block_ids": block_ids, "list_length": list_length, "w_query": w_query, "w_keyval": w_keyval, "w_out": w_out, "d_output": d_output}


def attend_block(query_block, footprint, live_count, grad_block):
    features = query_block.shape[1]
    heads = features // HD
    slots = footprint.shape[0] * footprint.shape[1]
    flat = footprint.reshape(slots, 2 * features)
    keys = flat[:, :features].reshape(slots, heads, HD).astype(jnp.float32)
    values = flat[:, features:].reshape(slots, heads, HD).astype(jnp.float32)
    queries = query_block.reshape(-1, heads, HD).astype(jnp.float32)
    slot_block = jnp.arange(slots, dtype=jnp.int32) // footprint.shape[1]
    live_slots = slot_block < live_count
    score_scale = HD ** -0.5
    scores = jnp.einsum("qhd,khd->hqk", queries, keys) * score_scale
    scores = jnp.where(live_slots[None, None, :], scores, -jnp.inf)
    top_score = jnp.max(scores, axis=-1, keepdims=True)
    raw_weights = jnp.exp(scores - top_score)
    probs = raw_weights / jnp.sum(raw_weights, axis=-1, keepdims=True)
    probs_low = lax.optimization_barrier(probs.astype(jnp.bfloat16)).astype(jnp.float32)
    attended = jnp.einsum("hqk,khd->qhd", probs_low, values).astype(jnp.bfloat16).reshape(-1, features)
    grads = grad_block.reshape(-1, heads, HD).astype(jnp.float32)
    d_probs = jnp.einsum("qhd,khd->hqk", grads, values)
    centre = jnp.sum(probs * d_probs, axis=-1, keepdims=True)
    d_scores = lax.optimization_barrier((probs * (d_probs - centre) * score_scale).astype(jnp.bfloat16)).astype(jnp.float32)
    d_queries = jnp.einsum("hqk,khd->qhd", d_scores, keys).astype(jnp.bfloat16).reshape(-1, features)
    d_keys = jnp.einsum("hqk,qhd->khd", d_scores, queries).reshape(slots, features)
    d_values = jnp.einsum("hqk,qhd->khd", probs_low, grads).reshape(slots, features)
    d_foot = jnp.concatenate([d_keys, d_values], axis=-1).reshape(footprint.shape[0], footprint.shape[1], 2 * features)
    return attended, d_queries, d_foot


def reference(nest_tokens, global_tokens, block_ids, list_length, w_query, w_keyval, w_out, d_output):
    queries = jnp.dot(nest_tokens, w_query, preferred_element_type=jnp.float32).astype(jnp.bfloat16)
    pairs = jnp.dot(global_tokens, w_keyval, preferred_element_type=jnp.float32).astype(jnp.bfloat16)
    pairs = pairs.reshape(GBLK, GB, 2 * D)
    grad_attn = jnp.dot(d_output, w_out.T, preferred_element_type=jnp.float32).astype(jnp.bfloat16)

    def visit(carry, inputs):
        query_block, row_ids, live_count, grad_block = inputs
        footprint = pairs[row_ids]
        attended, d_queries, d_foot = attend_block(query_block, footprint, live_count, grad_block)
        return carry.at[row_ids].add(d_foot), (attended, d_queries)

    start_pairs = jnp.zeros((GBLK, GB, 2 * D), jnp.float32)
    d_pairs, (attended, d_queries) = lax.scan(
        visit, start_pairs,
        (queries.reshape(NBLK, BT, D), block_ids, list_length, grad_attn.reshape(NBLK, BT, D)))
    attended = attended.reshape(NEST_TOKENS, D)
    d_queries = d_queries.reshape(NEST_TOKENS, D)
    d_pairs = d_pairs.reshape(GLOB_TOKENS, 2 * D)
    output = jnp.dot(attended, w_out, preferred_element_type=jnp.float32).astype(jnp.bfloat16)
    d_nest = jnp.dot(d_queries, w_query.T, preferred_element_type=jnp.float32).astype(jnp.bfloat16)
    d_global = jnp.dot(d_pairs, w_keyval.astype(jnp.float32).T, precision=lax.Precision.HIGHEST).astype(jnp.bfloat16)
    norm_factor = 1.0 / (NEST_TOKENS ** 0.5)
    grad_query = jnp.dot(nest_tokens.T, d_queries, preferred_element_type=jnp.float32) * norm_factor
    grad_keyval = jnp.dot(global_tokens.astype(jnp.float32).T, d_pairs, precision=lax.Precision.HIGHEST) * norm_factor
    grad_out = jnp.dot(attended.T, d_output, preferred_element_type=jnp.float32) * norm_factor
    return output, d_nest, d_global, grad_query, grad_keyval, grad_out
```

```python
import functools
import math

import jax
import jax.numpy as jnp
from jax import lax
from jax.experimental import pallas as pl
from jax.experimental.pallas import tpu as pltpu
from jax.sharding import PartitionSpec as P

HD = 32
BT = 128
GB = 128
LIST = 4
SUB = 16
F32 = jnp.float32
BF16 = jnp.bfloat16
VMEM_LIMIT = 56 * 1024 * 1024


def mm(a, b, ca=1, cb=0):
    return lax.dot_general(a, b, (((ca,), (cb,)), ((), ())), preferred_element_type=F32)


def coords():
    me = lax.axis_index("band")
    pos = me % SUB
    return me - pos, pos // 8, pos // 4 % 2, pos // 2 % 2, pos % 2


def partners(base, zh, zl, y, c):
    def at(a, b, d, e):
        return {"band": base + a * 8 + b * 4 + d * 2 + e}

    far = at(1 - zh, zl, y, c)
    near = at(zh, 1 - zl, y, c)
    side = at(zh, zl, 1 - y, c)
    core = at(zh, zl, y, 1 - c)
    return far, near, side, core


def greet(devices):
    barrier = pltpu.get_barrier_semaphore()
    for device in devices:
        pl.semaphore_signal(barrier, inc=1, device_id=device, device_id_type=pl.DeviceIdType.MESH)
    pl.semaphore_wait(barrier, len(devices))


def sender(send, recv):
    def copy(src, dst, k, device):
        op = pltpu.make_async_remote_copy(
            src_ref=src,
            dst_ref=dst,
            send_sem=send.at[k],
            recv_sem=recv.at[k],
            device_id=device,
            device_id_type=pl.DeviceIdType.MESH,
        )
        op.start()
        return op

    return copy


def gather_steps(buf, half, copy, first, at, to):
    zh, zl, y, c = at
    far, near, side, core = to
    lo, hi = pl.ds(0, half), pl.ds(half, half)

    def go(ref, k, device):
        return copy(ref, ref, first + k, device)

    ops = [go(buf.at[zh, zl, y, c], 0, far)]
    ops[0].wait_recv()
    ops.append(go(buf.at[:, zl, y, c, lo], 1, side))
    ops.append(go(buf.at[:, zl, y, c, hi], 2, near))
    ops[1].wait_recv()
    ops.append(go(buf.at[:, zl, :, c, lo], 3, near))
    ops[2].wait_recv()
    ops.append(go(buf.at[:, :, y, c, hi], 4, side))
    ops[3].wait_recv()
    ops[4].wait_recv()
    ops.append(go(buf.at[:, :, :, c], 5, core))
    ops[5].wait_recv()
    for op in ops:
        op.wait_send()


def gather_kernel(tok_ref, all_ref, send, recv):
    base, *at = coords()
    to = partners(base, *at)
    zh, zl, y, c = at
    all_ref[zh, zl, y, c] = tok_ref[...]
    greet(to)
    gather_steps(all_ref, tok_ref.shape[0] // 2, sender(send, recv), 0, at, to)


def attend_kernel(
    ids_ref, len_ref, tok_ref, nest_ref, dout_ref, wq_ref, wkv_ref, wo_ref,
    out_ref, dnest_ref, pay_ref,
    pairs, qs, gs, att, dq, dreg, foot, foot_t, qst, gst, pst, dst,
):
    feat = nest_ref.shape[1]
    slots = LIST * GB
    heads = feat // HD
    scale = HD ** (-0.5)
    for i in range(0, SUB * GB, slots):
        pairs[i : i + slots, :] = mm(tok_ref[i : i + slots, :], wkv_ref[...]).astype(BF16)
    dreg[...] = jnp.zeros_like(dreg)
    qs[...] = mm(nest_ref[...], wq_ref[...]).astype(BF16)
    gs[...] = mm(dout_ref[...], wo_ref[...], 1, 1).astype(BF16)
    head_of = lax.broadcasted_iota(jnp.int32, (BT, feat), 1) // HD
    slot_row = lax.broadcasted_iota(jnp.int32, (slots, 2 * BT), 0)

    def block(b, carry):
        rows = pl.ds(pl.multiple_of(b * BT, BT), BT)
        live = len_ref[b] * GB
        for j in range(LIST):
            start = pl.multiple_of(ids_ref[b, j] * GB, GB)
            foot[j * GB : (j + 1) * GB, :] = pairs[pl.ds(start, GB), :]
        foot_t[...] = foot[...].T
        q = qs[rows, :]
        g = gs[rows, :]
        zero = jnp.zeros_like(q)
        for h in range(heads):
            qst[h * BT : (h + 1) * BT, :] = jnp.where(head_of == h, q, zero)
            gst[h * BT : (h + 1) * BT, :] = jnp.where(head_of == h, g, zero)
        att_parts = []
        dq_parts = []
        for hp in range(heads // 2):
            two = slice(hp * 2 * BT, (hp + 1) * 2 * BT)
            s = mm(foot[:, :feat], qst[two, :], 1, 1)
            dp = mm(foot[:, feat:], gst[two, :], 1, 1)
            s = jnp.where(slot_row < live, s, -jnp.inf)
            top = jnp.max(s, axis=0, keepdims=True)
            e = jnp.exp2((s - top) * (scale * math.log2(math.e)))
            p = e * (1.0 / jnp.sum(e, axis=0, keepdims=True))
            p_low = p.astype(BF16)
            pst[:, two] = p_low
            centre = jnp.sum(p * dp, axis=0, keepdims=True)
            d_s = (p * (dp - centre) * scale).astype(BF16)
            dst[:, two] = d_s
            cols = slice(hp * 2 * HD, (hp + 1) * 2 * HD)
            vals = slice(feat + hp * 2 * HD, feat + (hp + 1) * 2 * HD)
            a_t = mm(foot_t[vals, :], p_low)
            q_t = mm(foot_t[cols, :], d_s)
            att_parts += [a_t[:HD, :BT], a_t[HD:, BT:]]
            dq_parts += [q_t[:HD, :BT], q_t[HD:, BT:]]
        att[rows, :] = jnp.concatenate(att_parts, axis=0).T.astype(BF16)
        dq[rows, :] = jnp.concatenate(dq_parts, axis=0).T.astype(BF16)
        d_k = mm(dst[...], qst[...])
        d_v = mm(pst[...], gst[...])
        for j in range(LIST):
            start = pl.multiple_of(ids_ref[b, j] * GB, GB)
            part = slice(j * GB, (j + 1) * GB)
            dreg[pl.ds(start, GB), :feat] += d_k[part, :]
            dreg[pl.ds(start, GB), feat:] += d_v[part, :]
        return carry

    lax.fori_loop(0, nest_ref.shape[0] // BT, block, 0)
    out_ref[...] = mm(att[...], wo_ref[...]).astype(BF16)
    dnest_ref[...] = mm(dq[...], wq_ref[...], 1, 1).astype(BF16)
    w_rows = 2 * feat // SUB
    kv = jnp.zeros((feat, 2 * feat), F32)
    for i in range(0, SUB * GB, slots):
        part = dreg[i : i + slots, :]
        high = part.astype(BF16)
        low = (part - high.astype(F32)).astype(BF16)
        tok = tok_ref[i : i + slots, :]
        kv = kv + mm(tok, high, 0, 0) + mm(tok, low, 0, 0)
        for g in range(LIST):
            pay_ref[i // GB + g, :GB, :] = high[g * GB : (g + 1) * GB, :]
    grad_q = mm(nest_ref[...], dq[...], 0, 0).astype(BF16)
    grad_o = mm(att[...], dout_ref[...], 0, 0).astype(BF16)
    kv = kv.astype(BF16)
    for k in range(SUB // 2):
        part = slice(k * w_rows, (k + 1) * w_rows)
        pay_ref[k, GB:, :] = kv[part, :]
        pay_ref[SUB // 2 + k, GB:, :feat] = grad_q[part, :]
        pay_ref[SUB // 2 + k, GB:, feat:] = grad_o[part, :]


def reduce_kernel(
    norm, pay_ref, wkv_ref, dglob_ref, gq_ref, gkv_ref, go_ref,
    ra, s0, s1, r0, r1, k0, k1, t0, t1, u0, u1, v0, v1, x0, x1, wg, send, recv,
):
    base, *at = coords()
    to = partners(base, *at)
    zh, zl, y, c = at
    far, near, side, core = to
    feat = wkv_ref.shape[0]
    greet(to)
    copy = sender(send, recv)
    left, right = pl.ds(0, feat), pl.ds(feat, feat)
    first = copy(pay_ref.at[:, :, :, 1 - c], ra, 0, core)
    first.wait_recv()
    s0[...] = (
        pay_ref[:, :, 1 - y, c, :, left].astype(F32) + ra[:, :, 1 - y, :, left].astype(F32)
    ).astype(BF16)
    b0 = copy(s0, r0, 1, side)
    s1[...] = (
        pay_ref[:, 1 - zl, :, c, :, right].astype(F32) + ra[:, 1 - zl, :, :, right].astype(F32)
    ).astype(BF16)
    b1 = copy(s1, r1, 2, near)
    k0[...] = pay_ref[:, :, y, c, :, left].astype(F32) + ra[:, :, y, :, left].astype(F32)
    k1[...] = pay_ref[:, zl, :, c, :, right].astype(F32) + ra[:, zl, :, :, right].astype(F32)
    b0.wait_recv()
    t0[...] = (k0[:, 1 - zl] + r0[:, 1 - zl].astype(F32)).astype(BF16)
    c0 = copy(t0, u0, 3, near)
    b1.wait_recv()
    t1[...] = (k1[:, 1 - y] + r1[:, 1 - y].astype(F32)).astype(BF16)
    c1 = copy(t1, u1, 4, side)
    c0.wait_recv()
    v0[...] = (
        k0[1 - zh, zl] + r0[1 - zh, zl].astype(F32) + u0[1 - zh].astype(F32)
    ).astype(BF16)
    d0 = copy(v0, x0, 5, far)
    c1.wait_recv()
    v1[...] = (
        k1[1 - zh, y] + r1[1 - zh, y].astype(F32) + u1[1 - zh].astype(F32)
    ).astype(BF16)
    d1 = copy(v1, x1, 6, far)
    sum0 = k0[zh, zl] + r0[zh, zl].astype(F32) + u0[zh].astype(F32)
    sum1 = k1[zh, y] + r1[zh, y].astype(F32) + u1[zh].astype(F32)
    d0.wait_recv()
    sum0 = sum0 + x0[...].astype(F32)
    wg[zh, zl, y, c, :, left] = sum0[GB:, :].astype(BF16)
    d1.wait_recv()
    sum1 = sum1 + x1[...].astype(F32)
    wg[zh, zl, y, c, :, right] = sum1[GB:, :].astype(BF16)
    total = jnp.zeros((GB, feat), F32)
    for part, cols in ((sum0[:GB, :], left), (sum1[:GB, :], right)):
        high = part.astype(BF16)
        low = (part - high.astype(F32)).astype(BF16)
        w = wkv_ref[:, cols]
        total = total + mm(high, w, 1, 1) + mm(low, w, 1, 1)
    dglob_ref[...] = total.astype(BF16)
    gather_steps(wg, wg.shape[4] // 2, copy, 7, at, to)
    flat = wg[...].astype(F32).reshape(2 * feat, 2 * feat) * norm
    gkv_ref[...] = flat[:feat, :]
    gq_ref[...] = flat[feat:, :feat]
    go_ref[...] = flat[feat:, feat:]
    for op in (first, b0, b1, c0, c1, d0, d1):
        op.wait_send()


def vmem(n):
    return [pl.BlockSpec(memory_space=pltpu.VMEM)] * n


def shards(nest_tokens, global_tokens, block_ids, list_length, w_query, w_keyval, w_out, d_output):
    rows, feat = nest_tokens.shape
    band = lax.axis_size("band")
    device = lax.axis_index("band")
    local_ids = block_ids - (device - device % SUB)
    norm = 1.0 / math.sqrt(rows * band)
    tokens = pl.pallas_call(
        gather_kernel,
        out_shape=jax.ShapeDtypeStruct((2, 2, 2, 2, GB, feat), BF16),
        in_specs=vmem(1),
        out_specs=vmem(1)[0],
        scratch_shapes=[pltpu.SemaphoreType.DMA((6,)), pltpu.SemaphoreType.DMA((6,))],
        compiler_params=pltpu.CompilerParams(
            collective_id=0, has_side_effects=True, vmem_limit_bytes=VMEM_LIMIT
        ),
    )(global_tokens)
    tokens = tokens.reshape(SUB * GB, feat)
    slots = LIST * GB
    wide = feat // HD * BT
    depth = GB + 2 * feat // SUB
    smem = [pl.BlockSpec(memory_space=pltpu.SMEM)] * 2
    output, d_nest, payload = pl.pallas_call(
        attend_kernel,
        out_shape=(
            jax.ShapeDtypeStruct((rows, feat), BF16),
            jax.ShapeDtypeStruct((rows, feat), BF16),
            jax.ShapeDtypeStruct((SUB, depth, 2 * feat), BF16),
        ),
        in_specs=smem + vmem(6),
        out_specs=tuple(vmem(3)),
        scratch_shapes=[
            pltpu.VMEM((SUB * GB, 2 * feat), BF16),
            pltpu.VMEM((rows, feat), BF16),
            pltpu.VMEM((rows, feat), BF16),
            pltpu.VMEM((rows, feat), BF16),
            pltpu.VMEM((rows, feat), BF16),
            pltpu.VMEM((SUB * GB, 2 * feat), F32),
            pltpu.VMEM((slots, 2 * feat), BF16),
            pltpu.VMEM((2 * feat, slots), BF16),
            pltpu.VMEM((wide, feat), BF16),
            pltpu.VMEM((wide, feat), BF16),
            pltpu.VMEM((slots, wide), BF16),
            pltpu.VMEM((slots, wide), BF16),
        ],
        compiler_params=pltpu.CompilerParams(vmem_limit_bytes=VMEM_LIMIT),
    )(local_ids, list_length, tokens, nest_tokens, d_output, w_query, w_keyval, w_out)
    payload = payload.reshape(2, 2, 2, 2, depth, 2 * feat)
    d_global, grad_q, grad_kv, grad_o = pl.pallas_call(
        functools.partial(reduce_kernel, norm),
        out_shape=(
            jax.ShapeDtypeStruct((GB, feat), BF16),
            jax.ShapeDtypeStruct((feat, feat), F32),
            jax.ShapeDtypeStruct((feat, 2 * feat), F32),
            jax.ShapeDtypeStruct((feat, feat), F32),
        ),
        in_specs=vmem(2),
        out_specs=tuple(vmem(4)),
        scratch_shapes=[
            pltpu.VMEM((2, 2, 2, depth, 2 * feat), BF16),
            pltpu.VMEM((2, 2, depth, feat), BF16),
            pltpu.VMEM((2, 2, depth, feat), BF16),
            pltpu.VMEM((2, 2, depth, feat), BF16),
            pltpu.VMEM((2, 2, depth, feat), BF16),
            pltpu.VMEM((2, 2, depth, feat), F32),
            pltpu.VMEM((2, 2, depth, feat), F32),
            pltpu.VMEM((2, depth, feat), BF16),
            pltpu.VMEM((2, depth, feat), BF16),
            pltpu.VMEM((2, depth, feat), BF16),
            pltpu.VMEM((2, depth, feat), BF16),
            pltpu.VMEM((depth, feat), BF16),
            pltpu.VMEM((depth, feat), BF16),
            pltpu.VMEM((depth, feat), BF16),
            pltpu.VMEM((depth, feat), BF16),
            pltpu.VMEM((2, 2, 2, 2, depth - GB, 2 * feat), BF16),
            pltpu.SemaphoreType.DMA((13,)),
            pltpu.SemaphoreType.DMA((13,)),
        ],
        compiler_params=pltpu.CompilerParams(
            collective_id=1, has_side_effects=True, vmem_limit_bytes=VMEM_LIMIT
        ),
    )(payload, w_keyval)
    if band > SUB:
        groups = [[s + SUB * k for k in range(band // SUB)] for s in range(SUB)]
        grad_q, grad_kv, grad_o = lax.psum(
            (grad_q, grad_kv, grad_o), "band", axis_index_groups=groups
        )
    return output, d_nest, d_global, grad_q, grad_kv, grad_o


def solution(mesh):
    both = ("groups", "band")
    in_specs = (
        P(both, None), P(both, None), P(both, None), P(both), P(), P(), P(), P(both, None),
    )
    out_specs = (
        P(both, None), P(both, None), P(both, None),
        P("groups", None), P("groups", None), P("groups", None),
    )
    return jax.shard_map(shards, mesh=mesh, in_specs=in_specs, out_specs=out_specs, check_vma=False)
```

```python
import functools
import math

import jax
import jax.numpy as jnp
from jax import lax
from jax.experimental import pallas as pl
from jax.experimental.pallas import tpu as pltpu
from jax.sharding import PartitionSpec as P

HD = 32
BT = 128
GB = 128
LIST = 4
SUB = 16
F32 = jnp.float32
BF16 = jnp.bfloat16
VMEM_LIMIT = 56 * 1024 * 1024


def mm(a, b, ca=1, cb=0):
    return lax.dot_general(a, b, (((ca,), (cb,)), ((), ())), preferred_element_type=F32)


def coords():
    me = lax.axis_index("band")
    pos = me % SUB
    return me - pos, pos // 8, pos // 4 % 2, pos // 2 % 2, pos % 2


def partners(base, zh, zl, y, c):
    def at(a, b, d, e):
        return {"band": base + a * 8 + b * 4 + d * 2 + e}

    far = at(1 - zh, zl, y, c)
    near = at(zh, 1 - zl, y, c)
    side = at(zh, zl, 1 - y, c)
    core = at(zh, zl, y, 1 - c)
    return far, near, side, core


def greet(devices):
    barrier = pltpu.get_barrier_semaphore()
    for device in devices:
        pl.semaphore_signal(barrier, inc=1, device_id=device, device_id_type=pl.DeviceIdType.MESH)
    pl.semaphore_wait(barrier, len(devices))


def sender(send, recv):
    def copy(src, dst, k, device):
        op = pltpu.make_async_remote_copy(
            src_ref=src,
            dst_ref=dst,
            send_sem=send.at[k],
            recv_sem=recv.at[k],
            device_id=device,
            device_id_type=pl.DeviceIdType.MESH,
        )
        op.start()
        return op

    return copy


def gather_steps(buf, half, copy, first, at, to, beside=None):
    zh, zl, y, c = at
    far, near, side, core = to
    lo, hi = pl.ds(0, half), pl.ds(half, half)

    def go(ref, k, device):
        return copy(ref, ref, first + k, device)

    ops = [go(buf.at[zh, zl, y, c], 0, far)]
    if beside is not None:
        beside()
    ops[0].wait_recv()
    ops.append(go(buf.at[:, zl, y, c, lo], 1, side))
    ops.append(go(buf.at[:, zl, y, c, hi], 2, near))
    ops[1].wait_recv()
    ops.append(go(buf.at[:, zl, :, c, lo], 3, near))
    ops[2].wait_recv()
    ops.append(go(buf.at[:, :, y, c, hi], 4, side))
    ops[3].wait_recv()
    ops[4].wait_recv()
    ops.append(go(buf.at[:, :, :, c], 5, core))
    ops[5].wait_recv()
    for op in ops:
        op.wait_send()


def gather_kernel(tok_ref, all_ref, send, recv):
    base, *at = coords()
    to = partners(base, *at)
    zh, zl, y, c = at
    all_ref[zh, zl, y, c] = tok_ref[...]
    greet(to)
    gather_steps(all_ref, tok_ref.shape[0] // 2, sender(send, recv), 0, at, to)


def attend_kernel(
    ids_ref, len_ref, tok_ref, nest_ref, dout_ref, wq_ref, wkv_ref, wo_ref,
    out_ref, dnest_ref, pay_ref,
    pairs, qs, gs, att, dq, dreg, foot, foot_t, qst, gst, pst, dst,
):
    feat = nest_ref.shape[1]
    slots = LIST * GB
    heads = feat // HD
    scale = HD ** (-0.5)
    for i in range(0, SUB * GB, slots):
        pairs[i : i + slots, :] = mm(tok_ref[i : i + slots, :], wkv_ref[...]).astype(BF16)
    dreg[...] = jnp.zeros_like(dreg)
    qs[...] = mm(nest_ref[...], wq_ref[...]).astype(BF16)
    gs[...] = mm(dout_ref[...], wo_ref[...], 1, 1).astype(BF16)
    head_of = lax.broadcasted_iota(jnp.int32, (BT, feat), 1) // HD
    slot_row = lax.broadcasted_iota(jnp.int32, (slots, 2 * BT), 0)

    def block(b, carry):
        rows = pl.ds(pl.multiple_of(b * BT, BT), BT)
        live = len_ref[b] * GB
        for j in range(LIST):
            start = pl.multiple_of(lax.rem(ids_ref[b, j], SUB) * GB, GB)
            foot[j * GB : (j + 1) * GB, :] = pairs[pl.ds(start, GB), :]
        foot_t[...] = foot[...].T
        q = qs[rows, :]
        g = gs[rows, :]
        zero = jnp.zeros_like(q)
        for h in range(heads):
            qst[h * BT : (h + 1) * BT, :] = jnp.where(head_of == h, q, zero)
            gst[h * BT : (h + 1) * BT, :] = jnp.where(head_of == h, g, zero)
        att_parts = []
        dq_parts = []
        for hp in range(heads // 2):
            two = slice(hp * 2 * BT, (hp + 1) * 2 * BT)
            s = mm(foot[:, :feat], qst[two, :], 1, 1)
            dp = mm(foot[:, feat:], gst[two, :], 1, 1)
            s = jnp.where(slot_row < live, s, -jnp.inf)
            top = jnp.max(s, axis=0, keepdims=True)
            e = jnp.exp2((s - top) * (scale * math.log2(math.e)))
            p = e * (1.0 / jnp.sum(e, axis=0, keepdims=True))
            p_low = p.astype(BF16)
            pst[:, two] = p_low
            centre = jnp.sum(p * dp, axis=0, keepdims=True)
            d_s = (p * (dp - centre) * scale).astype(BF16)
            dst[:, two] = d_s
            cols = slice(hp * 2 * HD, (hp + 1) * 2 * HD)
            vals = slice(feat + hp * 2 * HD, feat + (hp + 1) * 2 * HD)
            a_t = mm(foot_t[vals, :], p_low)
            q_t = mm(foot_t[cols, :], d_s)
            att_parts += [a_t[:HD, :BT], a_t[HD:, BT:]]
            dq_parts += [q_t[:HD, :BT], q_t[HD:, BT:]]
        att[rows, :] = jnp.concatenate(att_parts, axis=0).T.astype(BF16)
        dq[rows, :] = jnp.concatenate(dq_parts, axis=0).T.astype(BF16)
        d_k = mm(dst[...], qst[...])
        d_v = mm(pst[...], gst[...])
        for j in range(LIST):
            start = pl.multiple_of(lax.rem(ids_ref[b, j], SUB) * GB, GB)
            part = slice(j * GB, (j + 1) * GB)
            dreg[pl.ds(start, GB), :feat] += d_k[part, :]
            dreg[pl.ds(start, GB), feat:] += d_v[part, :]
        return carry

    lax.fori_loop(0, nest_ref.shape[0] // BT, block, 0)
    out_ref[...] = mm(att[...], wo_ref[...]).astype(BF16)
    dnest_ref[...] = mm(dq[...], wq_ref[...], 1, 1).astype(BF16)
    w_rows = 2 * feat // SUB
    kv = jnp.zeros((feat, 2 * feat), F32)
    for i in range(0, SUB * GB, slots):
        part = dreg[i : i + slots, :]
        high = part.astype(BF16)
        low = (part - high.astype(F32)).astype(BF16)
        tok = tok_ref[i : i + slots, :]
        kv = kv + mm(tok, high, 0, 0) + mm(tok, low, 0, 0)
        for g in range(LIST):
            for n in range(2 * feat // CH):
                pay_ref[n, i // GB + g, :GB, :] = high[
                    g * GB : (g + 1) * GB, n * CH : (n + 1) * CH
                ]
    grad_q = mm(nest_ref[...], dq[...], 0, 0).astype(BF16)
    grad_o = mm(att[...], dout_ref[...], 0, 0).astype(BF16)
    kv = kv.astype(BF16)
    per = feat // CH
    for k in range(SUB // 2):
        part = slice(k * w_rows, (k + 1) * w_rows)
        for n in range(2 * per):
            cols = slice(n % per * CH, (n % per + 1) * CH)
            pay_ref[n, k, GB:, :] = kv[part, n * CH : (n + 1) * CH]
            pay_ref[n, SUB // 2 + k, GB:, :] = (grad_q if n < per else grad_o)[part, cols]


CH = 128


def reduce_kernel(
    pay_ref, wkv_ref, dglob_ref, wg,
    ra, s_buf, r_buf, kept, t_buf, u_buf, v_buf, x_buf, own, send, recv,
):
    base, *at = coords()
    to = partners(base, *at)
    zh, zl, y, c = at
    far, near, side, core = to
    feat = wkv_ref.shape[0]
    chunks = pay_ref.shape[0]
    order = [k // 2 + k % 2 * (chunks // 2) for k in range(chunks)]
    greet(to)
    copy = sender(send, recv)
    ops = [copy(pay_ref.at[k, :, :, :, 1 - c], ra.at[k], k, core) for k in order]
    ops_a = dict(zip(order, ops))
    ops_b, ops_c, ops_d = {}, {}, {}
    for k in order:
        ops_a[k].wait_recv()
        if k < chunks // 2:
            sent = pay_ref[k, :, :, 1 - y, c].astype(F32) + ra[k, :, :, 1 - y].astype(F32)
            s_buf[k] = sent.astype(BF16)
            ops_b[k] = copy(s_buf.at[k], r_buf.at[k], chunks + k, side)
            kept[k] = pay_ref[k, :, :, y, c].astype(F32) + ra[k, :, :, y].astype(F32)
        else:
            sent = pay_ref[k, :, 1 - zl, :, c].astype(F32) + ra[k, :, 1 - zl].astype(F32)
            s_buf[k] = sent.astype(BF16)
            ops_b[k] = copy(s_buf.at[k], r_buf.at[k], chunks + k, near)
            kept[k] = pay_ref[k, :, zl, :, c].astype(F32) + ra[k, :, zl].astype(F32)
    for k in order:
        mine, there = (zl, near) if k < chunks // 2 else (y, side)
        ops_b[k].wait_recv()
        t_buf[k] = (kept[k, :, 1 - mine] + r_buf[k, :, 1 - mine].astype(F32)).astype(BF16)
        ops_c[k] = copy(t_buf.at[k], u_buf.at[k], 2 * chunks + k, there)
    for k in order:
        mine = zl if k < chunks // 2 else y
        ops_c[k].wait_recv()
        v_buf[k] = (
            kept[k, 1 - zh, mine] + r_buf[k, 1 - zh, mine].astype(F32) + u_buf[k, 1 - zh].astype(F32)
        ).astype(BF16)
        ops_d[k] = copy(v_buf.at[k], x_buf.at[k], 3 * chunks + k, far)
    for k in order:
        mine = zl if k < chunks // 2 else y
        part = kept[k, zh, mine] + r_buf[k, zh, mine].astype(F32) + u_buf[k, zh].astype(F32)
        ops_d[k].wait_recv()
        part = part + x_buf[k].astype(F32)
        wg[zh, zl, y, c, :, k * CH : (k + 1) * CH] = part[GB:, :].astype(BF16)
        own[:, k * CH : (k + 1) * CH] = part[:GB, :]

    def finish():
        part = own[...]
        high = part.astype(BF16)
        low = (part - high.astype(F32)).astype(BF16)
        total = mm(high, wkv_ref[...], 1, 1) + mm(low, wkv_ref[...], 1, 1)
        dglob_ref[...] = total.astype(BF16)

    gather_steps(wg, wg.shape[4] // 2, copy, 4 * chunks, at, to, finish)
    for group in (ops_a, ops_b, ops_c, ops_d):
        for k in order:
            group[k].wait_send()


def finish_kernel(norm, dglob_in, wg_ref, dglob_ref, gq_ref, gkv_ref, go_ref):
    feat = gq_ref.shape[0]
    dglob_ref[...] = dglob_in[...]
    gkv_ref[...] = wg_ref[:feat, :].astype(F32) * norm
    gq_ref[...] = wg_ref[feat:, :feat].astype(F32) * norm
    go_ref[...] = wg_ref[feat:, feat:].astype(F32) * norm


def vmem(n):
    return [pl.BlockSpec(memory_space=pltpu.VMEM)] * n


def shards(nest_tokens, global_tokens, block_ids, list_length, w_query, w_keyval, w_out, d_output):
    rows, feat = nest_tokens.shape
    band = lax.axis_size("band")
    norm = 1.0 / math.sqrt(rows * band)
    tokens = pl.pallas_call(
        gather_kernel,
        out_shape=jax.ShapeDtypeStruct((2, 2, 2, 2, GB, feat), BF16),
        in_specs=vmem(1),
        out_specs=vmem(1)[0],
        scratch_shapes=[pltpu.SemaphoreType.DMA((6,)), pltpu.SemaphoreType.DMA((6,))],
        compiler_params=pltpu.CompilerParams(
            collective_id=0, has_side_effects=True, vmem_limit_bytes=VMEM_LIMIT
        ),
    )(global_tokens)
    tokens = tokens.reshape(SUB * GB, feat)
    slots = LIST * GB
    wide = feat // HD * BT
    depth = GB + 2 * feat // SUB
    smem = [pl.BlockSpec(memory_space=pltpu.SMEM)] * 2
    output, d_nest, payload = pl.pallas_call(
        attend_kernel,
        out_shape=(
            jax.ShapeDtypeStruct((rows, feat), BF16),
            jax.ShapeDtypeStruct((rows, feat), BF16),
            jax.ShapeDtypeStruct((2 * feat // CH, SUB, depth, CH), BF16),
        ),
        in_specs=smem + vmem(6),
        out_specs=tuple(vmem(3)),
        scratch_shapes=[
            pltpu.VMEM((SUB * GB, 2 * feat), BF16),
            pltpu.VMEM((rows, feat), BF16),
            pltpu.VMEM((rows, feat), BF16),
            pltpu.VMEM((rows, feat), BF16),
            pltpu.VMEM((rows, feat), BF16),
            pltpu.VMEM((SUB * GB, 2 * feat), F32),
            pltpu.VMEM((slots, 2 * feat), BF16),
            pltpu.VMEM((2 * feat, slots), BF16),
            pltpu.VMEM((wide, feat), BF16),
            pltpu.VMEM((wide, feat), BF16),
            pltpu.VMEM((slots, wide), BF16),
            pltpu.VMEM((slots, wide), BF16),
        ],
        compiler_params=pltpu.CompilerParams(vmem_limit_bytes=VMEM_LIMIT),
    )(block_ids, list_length, tokens, nest_tokens, d_output, w_query, w_keyval, w_out)
    n = 2 * feat // CH
    payload = payload.reshape(n, 2, 2, 2, 2, depth, CH)
    d_global, sums = pl.pallas_call(
        reduce_kernel,
        out_shape=(
            jax.ShapeDtypeStruct((GB, feat), BF16),
            jax.ShapeDtypeStruct((2, 2, 2, 2, depth - GB, 2 * feat), BF16),
        ),
        in_specs=vmem(2),
        out_specs=tuple(vmem(2)),
        scratch_shapes=[
            pltpu.VMEM((n, 2, 2, 2, depth, CH), BF16),
            pltpu.VMEM((n, 2, 2, depth, CH), BF16),
            pltpu.VMEM((n, 2, 2, depth, CH), BF16),
            pltpu.VMEM((n, 2, 2, depth, CH), F32),
            pltpu.VMEM((n, 2, depth, CH), BF16),
            pltpu.VMEM((n, 2, depth, CH), BF16),
            pltpu.VMEM((n, depth, CH), BF16),
            pltpu.VMEM((n, depth, CH), BF16),
            pltpu.VMEM((GB, 2 * feat), F32),
            pltpu.SemaphoreType.DMA((4 * n + 6,)),
            pltpu.SemaphoreType.DMA((4 * n + 6,)),
        ],
        compiler_params=pltpu.CompilerParams(
            collective_id=1, has_side_effects=True, vmem_limit_bytes=VMEM_LIMIT
        ),
    )(payload, w_keyval)
    d_global, grad_q, grad_kv, grad_o = pl.pallas_call(
        functools.partial(finish_kernel, norm),
        out_shape=(
            jax.ShapeDtypeStruct((GB, feat), BF16),
            jax.ShapeDtypeStruct((feat, feat), F32),
            jax.ShapeDtypeStruct((feat, 2 * feat), F32),
            jax.ShapeDtypeStruct((feat, feat), F32),
        ),
        in_specs=vmem(2),
        out_specs=tuple(vmem(4)),
        compiler_params=pltpu.CompilerParams(vmem_limit_bytes=VMEM_LIMIT),
    )(d_global, sums.reshape(2 * feat, 2 * feat))
    if band > SUB:
        groups = [[s + SUB * k for k in range(band // SUB)] for s in range(SUB)]
        grad_q, grad_kv, grad_o = lax.psum(
            (grad_q, grad_kv, grad_o), "band", axis_index_groups=groups
        )
    return output, d_nest, d_global, grad_q, grad_kv, grad_o


def solution(mesh):
    both = ("groups", "band")
    in_specs = (
        P(both, None), P(both, None), P(both, None), P(both), P(), P(), P(), P(both, None),
    )
    out_specs = (
        P(both, None), P(both, None), P(both, None),
        P("groups", None), P("groups", None), P("groups", None),
    )
    return jax.shard_map(shards, mesh=mesh, in_specs=in_specs, out_specs=out_specs, check_vma=False)
```

```python
import functools
import math

import jax
import jax.numpy as jnp
from jax import lax
from jax.experimental import pallas as pl
from jax.experimental.pallas import tpu as pltpu
from jax.sharding import PartitionSpec as P

HD = 32
BT = 128
GB = 128
LIST = 4
SUB = 16
F32 = jnp.float32
BF16 = jnp.bfloat16
VMEM_LIMIT = 56 * 1024 * 1024


def mm(a, b, ca=1, cb=0):
    return lax.dot_general(a, b, (((ca,), (cb,)), ((), ())), preferred_element_type=F32)


def coords():
    me = lax.axis_index("band")
    pos = me % SUB
    return me - pos, pos // 8, pos // 4 % 2, pos // 2 % 2, pos % 2


def partners(base, zh, zl, y, c):
    def at(a, b, d, e):
        return {"band": base + a * 8 + b * 4 + d * 2 + e}

    far = at(1 - zh, zl, y, c)
    near = at(zh, 1 - zl, y, c)
    side = at(zh, zl, 1 - y, c)
    core = at(zh, zl, y, 1 - c)
    return far, near, side, core


def greet(devices):
    barrier = pltpu.get_barrier_semaphore()
    for device in devices:
        pl.semaphore_signal(barrier, inc=1, device_id=device, device_id_type=pl.DeviceIdType.MESH)
    pl.semaphore_wait(barrier, len(devices))


def sender(send, recv):
    def copy(src, dst, k, device):
        op = pltpu.make_async_remote_copy(
            src_ref=src,
            dst_ref=dst,
            send_sem=send.at[k],
            recv_sem=recv.at[k],
            device_id=device,
            device_id_type=pl.DeviceIdType.MESH,
        )
        op.start()
        return op

    return copy


def gather_steps(buf, half, copy, first, at, to):
    zh, zl, y, c = at
    far, near, side, core = to
    lo, hi = pl.ds(0, half), pl.ds(half, half)

    def go(ref, k, device):
        return copy(ref, ref, first + k, device)

    ops = [go(buf.at[zh, zl, y, c], 0, far)]
    yield
    ops[0].wait_recv()
    ops.append(go(buf.at[:, zl, y, c, lo], 1, side))
    ops.append(go(buf.at[:, zl, y, c, hi], 2, near))
    yield
    ops[1].wait_recv()
    ops.append(go(buf.at[:, zl, :, c, lo], 3, near))
    ops[2].wait_recv()
    ops.append(go(buf.at[:, :, y, c, hi], 4, side))
    yield
    ops[3].wait_recv()
    ops[4].wait_recv()
    ops.append(go(buf.at[:, :, :, c], 5, core))
    yield
    ops[5].wait_recv()
    for op in ops:
        op.wait_send()
    yield


def halve_steps(side_first, pay, bufs, copy, k, at, to, done):
    ra, s_buf, r_buf, kept, t_buf, u_buf, v_buf, x_buf = bufs
    zh, zl, y, c = at
    far, near, side, core = to
    ops = [copy(pay.at[:, :, :, 1 - c], ra, k, core)]
    yield
    ops[0].wait_recv()
    if side_first:
        sent = pay[:, :, 1 - y, c].astype(F32) + ra[:, :, 1 - y].astype(F32)
    else:
        sent = pay[:, 1 - zl, :, c].astype(F32) + ra[:, 1 - zl].astype(F32)
    s_buf[...] = sent.astype(BF16)
    ops.append(copy(s_buf, r_buf, k + 1, side if side_first else near))
    if side_first:
        kept[...] = pay[:, :, y, c].astype(F32) + ra[:, :, y].astype(F32)
    else:
        kept[...] = pay[:, zl, :, c].astype(F32) + ra[:, zl].astype(F32)
    mine = zl if side_first else y
    yield
    ops[1].wait_recv()
    t_buf[...] = (kept[:, 1 - mine] + r_buf[:, 1 - mine].astype(F32)).astype(BF16)
    ops.append(copy(t_buf, u_buf, k + 2, near if side_first else side))
    yield
    ops[2].wait_recv()
    v_buf[...] = (
        kept[1 - zh, mine] + r_buf[1 - zh, mine].astype(F32) + u_buf[1 - zh].astype(F32)
    ).astype(BF16)
    ops.append(copy(v_buf, x_buf, k + 3, far))
    yield
    ops[3].wait_recv()
    part = kept[zh, mine] + r_buf[zh, mine].astype(F32) + u_buf[zh].astype(F32)
    done(part + x_buf[...].astype(F32))
    yield
    for op in ops:
        op.wait_send()
    yield


def gather_kernel(tok_ref, all_ref, send, recv):
    base, *at = coords()
    to = partners(base, *at)
    zh, zl, y, c = at
    all_ref[zh, zl, y, c] = tok_ref[...]
    greet(to)
    for _ in gather_steps(all_ref, tok_ref.shape[0] // 2, sender(send, recv), 0, at, to):
        pass


def attend_kernel(
    ids_ref, len_ref, tok_ref, nest_ref, dout_ref, wq_ref, wkv_ref, wo_ref,
    out_ref, dnest_ref, pay_ref, wpay_ref,
    pairs, qs, gs, att, dq, dreg, foot, foot_t, qst, gst, pst, dst,
):
    feat = nest_ref.shape[1]
    slots = LIST * GB
    heads = feat // HD
    scale = HD ** (-0.5)
    for i in range(0, SUB * GB, slots):
        pairs[i : i + slots, :] = mm(tok_ref[i : i + slots, :], wkv_ref[...]).astype(BF16)
    dreg[...] = jnp.zeros_like(dreg)
    qs[...] = mm(nest_ref[...], wq_ref[...]).astype(BF16)
    gs[...] = mm(dout_ref[...], wo_ref[...], 1, 1).astype(BF16)
    head_of = lax.broadcasted_iota(jnp.int32, (BT, feat), 1) // HD
    slot_row = lax.broadcasted_iota(jnp.int32, (slots, 2 * BT), 0)

    def block(b, carry):
        rows = pl.ds(pl.multiple_of(b * BT, BT), BT)
        live = len_ref[b] * GB
        for j in range(LIST):
            start = pl.multiple_of(lax.rem(ids_ref[b, j], SUB) * GB, GB)
            foot[j * GB : (j + 1) * GB, :] = pairs[pl.ds(start, GB), :]
        foot_t[...] = foot[...].T
        q = qs[rows, :]
        g = gs[rows, :]
        zero = jnp.zeros_like(q)
        for h in range(heads):
            qst[h * BT : (h + 1) * BT, :] = jnp.where(head_of == h, q, zero)
            gst[h * BT : (h + 1) * BT, :] = jnp.where(head_of == h, g, zero)
        att_parts = []
        dq_parts = []
        for hp in range(heads // 2):
            two = slice(hp * 2 * BT, (hp + 1) * 2 * BT)
            s = mm(foot[:, :feat], qst[two, :], 1, 1)
            dp = mm(foot[:, feat:], gst[two, :], 1, 1)
            s = jnp.where(slot_row < live, s, -jnp.inf)
            top = jnp.max(s, axis=0, keepdims=True)
            e = jnp.exp2((s - top) * (scale * math.log2(math.e)))
            p = e * (1.0 / jnp.sum(e, axis=0, keepdims=True))
            p_low = p.astype(BF16)
            pst[:, two] = p_low
            centre = jnp.sum(p * dp, axis=0, keepdims=True)
            d_s = (p * (dp - centre) * scale).astype(BF16)
            dst[:, two] = d_s
            cols = slice(hp * 2 * HD, (hp + 1) * 2 * HD)
            vals = slice(feat + hp * 2 * HD, feat + (hp + 1) * 2 * HD)
            a_t = mm(foot_t[vals, :], p_low)
            q_t = mm(foot_t[cols, :], d_s)
            att_parts += [a_t[:HD, :BT], a_t[HD:, BT:]]
            dq_parts += [q_t[:HD, :BT], q_t[HD:, BT:]]
        att[rows, :] = jnp.concatenate(att_parts, axis=0).T.astype(BF16)
        dq[rows, :] = jnp.concatenate(dq_parts, axis=0).T.astype(BF16)
        d_k = mm(dst[...], qst[...])
        d_v = mm(pst[...], gst[...])
        for j in range(LIST):
            start = pl.multiple_of(lax.rem(ids_ref[b, j], SUB) * GB, GB)
            part = slice(j * GB, (j + 1) * GB)
            dreg[pl.ds(start, GB), :feat] += d_k[part, :]
            dreg[pl.ds(start, GB), feat:] += d_v[part, :]
        return carry

    lax.fori_loop(0, nest_ref.shape[0] // BT, block, 0)
    out_ref[...] = mm(att[...], wo_ref[...]).astype(BF16)
    dnest_ref[...] = mm(dq[...], wq_ref[...], 1, 1).astype(BF16)
    w_rows = 2 * feat // SUB
    kv = jnp.zeros((feat, 2 * feat), F32)
    for i in range(0, SUB * GB, slots):
        part = dreg[i : i + slots, :]
        high = part.astype(BF16)
        low = (part - high.astype(F32)).astype(BF16)
        tok = tok_ref[i : i + slots, :]
        kv = kv + mm(tok, high, 0, 0) + mm(tok, low, 0, 0)
        for g in range(LIST):
            for n in range(2 * feat // CH):
                pay_ref[n, i // GB + g] = high[
                    g * GB : (g + 1) * GB, n * CH : (n + 1) * CH
                ]
    grad_q = mm(nest_ref[...], dq[...], 0, 0).astype(BF16)
    grad_o = mm(att[...], dout_ref[...], 0, 0).astype(BF16)
    kv = kv.astype(BF16)
    for k in range(SUB // 2):
        part = slice(k * w_rows, (k + 1) * w_rows)
        wpay_ref[0, k] = kv[part, :feat]
        wpay_ref[1, k] = kv[part, feat:]
        wpay_ref[0, SUB // 2 + k] = grad_q[part, :]
        wpay_ref[1, SUB // 2 + k] = grad_o[part, :]


CH = 128


def reduce_kernel(pay_ref, wpay_ref, wkv_ref, dglob_ref, wg, *rest):
    pair_bufs, weight_bufs, (own, send, recv) = rest[:8], rest[8:16], rest[16:]
    base, *at = coords()
    to = partners(base, *at)
    zh, zl, y, c = at
    feat = wkv_ref.shape[0]
    chunks = pay_ref.shape[0]
    greet(to)
    copy = sender(send, recv)

    def keep_pairs(k):
        def done(total):
            own[:, k * CH : (k + 1) * CH] = total

        return done

    def keep_weights(k):
        def done(total):
            wg[zh, zl, y, c, :, k * feat : (k + 1) * feat] = total.astype(BF16)

        return done

    steps = {}
    for k in range(2):
        bufs = [buf.at[k] for buf in weight_bufs]
        steps["w", k] = halve_steps(
            k == 0, wpay_ref.at[k], bufs, copy, 4 * k, at, to, keep_weights(k)
        )
    for k in range(chunks):
        bufs = [buf.at[k] for buf in pair_bufs]
        steps["p", k] = halve_steps(
            k < chunks // 2, pay_ref.at[k], bufs, copy, 8 + 4 * k, at, to, keep_pairs(k)
        )
    share = gather_steps(wg, wg.shape[4] // 2, copy, 8 + 4 * chunks, at, to)

    def weights():
        for k in range(2):
            next(steps["w", k])

    def pairs(first):
        for k in range(first, chunks // 2, 2):
            next(steps["p", k])
            next(steps["p", k + chunks // 2])

    weights()
    pairs(0)
    pairs(1)
    weights()
    pairs(0)
    weights()
    pairs(1)
    weights()
    pairs(0)
    weights()
    next(share)
    pairs(1)
    next(share)
    pairs(0)
    next(share)
    pairs(1)
    next(share)
    pairs(0)
    pairs(1)
    part = own[...]
    high = part.astype(BF16)
    low = (part - high.astype(F32)).astype(BF16)
    total = mm(high, wkv_ref[...], 1, 1) + mm(low, wkv_ref[...], 1, 1)
    dglob_ref[...] = total.astype(BF16)
    next(share)
    weights()
    pairs(0)
    pairs(1)


def finish_kernel(norm, dglob_in, wg_ref, dglob_ref, gq_ref, gkv_ref, go_ref):
    feat = gq_ref.shape[0]
    dglob_ref[...] = dglob_in[...]
    gkv_ref[...] = wg_ref[:feat, :].astype(F32) * norm
    gq_ref[...] = wg_ref[feat:, :feat].astype(F32) * norm
    go_ref[...] = wg_ref[feat:, feat:].astype(F32) * norm


def vmem(n):
    return [pl.BlockSpec(memory_space=pltpu.VMEM)] * n


def shards(nest_tokens, global_tokens, block_ids, list_length, w_query, w_keyval, w_out, d_output):
    rows, feat = nest_tokens.shape
    band = lax.axis_size("band")
    norm = 1.0 / math.sqrt(rows * band)
    tokens = pl.pallas_call(
        gather_kernel,
        out_shape=jax.ShapeDtypeStruct((2, 2, 2, 2, GB, feat), BF16),
        in_specs=vmem(1),
        out_specs=vmem(1)[0],
        scratch_shapes=[pltpu.SemaphoreType.DMA((6,)), pltpu.SemaphoreType.DMA((6,))],
        compiler_params=pltpu.CompilerParams(
            collective_id=0, has_side_effects=True, vmem_limit_bytes=VMEM_LIMIT
        ),
    )(global_tokens)
    tokens = tokens.reshape(SUB * GB, feat)
    slots = LIST * GB
    wide = feat // HD * BT
    few = 2 * feat // SUB
    smem = [pl.BlockSpec(memory_space=pltpu.SMEM)] * 2
    output, d_nest, payload, wide_payload = pl.pallas_call(
        attend_kernel,
        out_shape=(
            jax.ShapeDtypeStruct((rows, feat), BF16),
            jax.ShapeDtypeStruct((rows, feat), BF16),
            jax.ShapeDtypeStruct((2 * feat // CH, SUB, GB, CH), BF16),
            jax.ShapeDtypeStruct((2, SUB, few, feat), BF16),
        ),
        in_specs=smem + vmem(6),
        out_specs=tuple(vmem(4)),
        scratch_shapes=[
            pltpu.VMEM((SUB * GB, 2 * feat), BF16),
            pltpu.VMEM((rows, feat), BF16),
            pltpu.VMEM((rows, feat), BF16),
            pltpu.VMEM((rows, feat), BF16),
            pltpu.VMEM((rows, feat), BF16),
            pltpu.VMEM((SUB * GB, 2 * feat), F32),
            pltpu.VMEM((slots, 2 * feat), BF16),
            pltpu.VMEM((2 * feat, slots), BF16),
            pltpu.VMEM((wide, feat), BF16),
            pltpu.VMEM((wide, feat), BF16),
            pltpu.VMEM((slots, wide), BF16),
            pltpu.VMEM((slots, wide), BF16),
        ],
        compiler_params=pltpu.CompilerParams(vmem_limit_bytes=VMEM_LIMIT),
    )(block_ids, list_length, tokens, nest_tokens, d_output, w_query, w_keyval, w_out)
    n = 2 * feat // CH
    payload = payload.reshape(n, 2, 2, 2, 2, GB, CH)
    wide_payload = wide_payload.reshape(2, 2, 2, 2, 2, few, feat)
    scratch = []
    for count, block in ((n, (GB, CH)), (2, (few, feat))):
        for lead, dtype in (
            ((2, 2, 2), BF16), ((2, 2), BF16), ((2, 2), BF16), ((2, 2), F32),
            ((2,), BF16), ((2,), BF16), ((), BF16), ((), BF16),
        ):
            scratch.append(pltpu.VMEM((count, *lead, *block), dtype))
    copies = 8 + 4 * n + 6
    d_global, sums = pl.pallas_call(
        reduce_kernel,
        out_shape=(
            jax.ShapeDtypeStruct((GB, feat), BF16),
            jax.ShapeDtypeStruct((2, 2, 2, 2, few, 2 * feat), BF16),
        ),
        in_specs=vmem(3),
        out_specs=tuple(vmem(2)),
        scratch_shapes=scratch + [
            pltpu.VMEM((GB, 2 * feat), F32),
            pltpu.SemaphoreType.DMA((copies,)),
            pltpu.SemaphoreType.DMA((copies,)),
        ],
        compiler_params=pltpu.CompilerParams(
            collective_id=1, has_side_effects=True, vmem_limit_bytes=VMEM_LIMIT
        ),
    )(payload, wide_payload, w_keyval)
    d_global, grad_q, grad_kv, grad_o = pl.pallas_call(
        functools.partial(finish_kernel, norm),
        out_shape=(
            jax.ShapeDtypeStruct((GB, feat), BF16),
            jax.ShapeDtypeStruct((feat, feat), F32),
            jax.ShapeDtypeStruct((feat, 2 * feat), F32),
            jax.ShapeDtypeStruct((feat, feat), F32),
        ),
        in_specs=vmem(2),
        out_specs=tuple(vmem(4)),
        compiler_params=pltpu.CompilerParams(vmem_limit_bytes=VMEM_LIMIT),
    )(d_global, sums.reshape(2 * feat, 2 * feat))
    if band > SUB:
        groups = [[s + SUB * k for k in range(band // SUB)] for s in range(SUB)]
        grad_q, grad_kv, grad_o = lax.psum(
            (grad_q, grad_kv, grad_o), "band", axis_index_groups=groups
        )
    return output, d_nest, d_global, grad_q, grad_kv, grad_o


def solution(mesh):
    both = ("groups", "band")
    in_specs = (
        P(both, None), P(both, None), P(both, None), P(both), P(), P(), P(), P(both, None),
    )
    out_specs = (
        P(both, None), P(both, None), P(both, None),
        P("groups", None), P("groups", None), P("groups", None),
    )
    return jax.shard_map(shards, mesh=mesh, in_specs=in_specs, out_specs=out_specs, check_vma=False)
```

```python
import functools
import math

import jax
import jax.numpy as jnp
from jax import lax
from jax.experimental import pallas as pl
from jax.experimental.pallas import tpu as pltpu
from jax.sharding import PartitionSpec as P

HD = 32
BT = 128
GB = 128
LIST = 4
SUB = 16
F32 = jnp.float32
BF16 = jnp.bfloat16
VMEM_LIMIT = 30 * 1024 * 1024


def mm(a, b, ca=1, cb=0):
    return lax.dot_general(a, b, (((ca,), (cb,)), ((), ())), preferred_element_type=F32)


def coords():
    me = lax.axis_index("band")
    pos = me % SUB
    return me - pos, pos // 8, pos // 4 % 2, pos // 2 % 2, pos % 2


def partners(base, zh, zl, y, c):
    def at(a, b, d, e):
        return {"band": base + a * 8 + b * 4 + d * 2 + e}

    far = at(1 - zh, zl, y, c)
    near = at(zh, 1 - zl, y, c)
    side = at(zh, zl, 1 - y, c)
    core = at(zh, zl, y, 1 - c)
    return far, near, side, core


def greet(devices):
    barrier = pltpu.get_barrier_semaphore()
    for device in devices:
        pl.semaphore_signal(barrier, inc=1, device_id=device, device_id_type=pl.DeviceIdType.MESH)
    pl.semaphore_wait(barrier, len(devices))


def sender(send, recv):
    def copy(src, dst, k, device):
        op = pltpu.make_async_remote_copy(
            src_ref=src,
            dst_ref=dst,
            send_sem=send.at[k],
            recv_sem=recv.at[k],
            device_id=device,
            device_id_type=pl.DeviceIdType.MESH,
        )
        op.start()
        return op

    return copy


def gather_steps(buf, half, copy, first, at, to):
    zh, zl, y, c = at
    far, near, side, core = to
    lo, hi = pl.ds(0, half), pl.ds(half, half)

    def go(ref, k, device):
        return copy(ref, ref, first + k, device)

    ops = [go(buf.at[zh, zl, y, c], 0, far)]
    yield
    ops[0].wait_recv()
    ops.append(go(buf.at[:, zl, y, c, lo], 1, side))
    ops.append(go(buf.at[:, zl, y, c, hi], 2, near))
    yield
    ops[1].wait_recv()
    ops.append(go(buf.at[:, zl, :, c, lo], 3, near))
    ops[2].wait_recv()
    ops.append(go(buf.at[:, :, y, c, hi], 4, side))
    yield
    ops[3].wait_recv()
    ops[4].wait_recv()
    ops.append(go(buf.at[:, :, :, c], 5, core))
    yield
    ops[5].wait_recv()
    for op in ops:
        op.wait_send()
    yield


def halve_steps(side_first, pay, bufs, copy, k, at, to, done):
    ra, s_buf, r_buf, kept, t_buf, u_buf, v_buf, x_buf = bufs
    zh, zl, y, c = at
    far, near, side, core = to
    ops = [copy(pay.at[:, :, :, 1 - c], ra, k, core)]
    yield
    ops[0].wait_recv()
    if side_first:
        sent = pay[:, :, 1 - y, c].astype(F32) + ra[:, :, 1 - y].astype(F32)
    else:
        sent = pay[:, 1 - zl, :, c].astype(F32) + ra[:, 1 - zl].astype(F32)
    s_buf[...] = sent.astype(BF16)
    ops.append(copy(s_buf, r_buf, k + 1, side if side_first else near))
    if side_first:
        kept[...] = pay[:, :, y, c].astype(F32) + ra[:, :, y].astype(F32)
    else:
        kept[...] = pay[:, zl, :, c].astype(F32) + ra[:, zl].astype(F32)
    mine = zl if side_first else y
    yield
    ops[1].wait_recv()
    t_buf[...] = (kept[:, 1 - mine] + r_buf[:, 1 - mine].astype(F32)).astype(BF16)
    ops.append(copy(t_buf, u_buf, k + 2, near if side_first else side))
    yield
    ops[2].wait_recv()
    v_buf[...] = (
        kept[1 - zh, mine] + r_buf[1 - zh, mine].astype(F32) + u_buf[1 - zh].astype(F32)
    ).astype(BF16)
    ops.append(copy(v_buf, x_buf, k + 3, far))
    yield
    ops[3].wait_recv()
    part = kept[zh, mine] + r_buf[zh, mine].astype(F32) + u_buf[zh].astype(F32)
    done(part + x_buf[...].astype(F32))
    yield
    for op in ops:
        op.wait_send()
    yield


def spread_steps(side_first, buf, rows, copy, k, at, to):
    zh, zl, y, c = at
    far, near, side, core = to

    def go(ref, device):
        ops.append(copy(ref, ref, k + len(ops), device))

    ops = []
    go(buf.at[zh, zl, y, c, rows], far)
    yield
    ops[0].wait_recv()
    go(buf.at[:, zl, y, c, rows], side if side_first else near)
    yield
    ops[1].wait_recv()
    if side_first:
        go(buf.at[:, zl, :, c, rows], near)
    else:
        go(buf.at[:, :, y, c, rows], side)
    yield
    ops[2].wait_recv()
    go(buf.at[:, :, :, c, rows], core)
    yield
    ops[3].wait_recv()
    for op in ops:
        op.wait_send()
    yield


PIECES = 4


def gather_kernel(tok_ref, all_ref, send, recv):
    base, *at = coords()
    to = partners(base, *at)
    zh, zl, y, c = at
    all_ref[zh, zl, y, c] = tok_ref[...]
    greet(to)
    copy = sender(send, recv)
    size = tok_ref.shape[0] // PIECES
    steps = [
        spread_steps(k % 2 == 0, all_ref, pl.ds(k * size, size), copy, 4 * k, at, to)
        for k in range(PIECES)
    ]
    for _ in range(5):
        for step in steps:
            next(step)


def attend_kernel(
    ids_ref, len_ref, tok_ref, nest_ref, dout_ref, wq_ref, wkv_ref, wo_ref,
    out_ref, dnest_ref, pay_ref, wpay_ref,
    pairs, qs, gs, att, dq, dreg, foot, foot_t, qst, gst, pst, dst,
):
    feat = nest_ref.shape[1]
    slots = LIST * GB
    heads = feat // HD
    scale = HD ** (-0.5)
    for i in range(0, SUB * GB, slots):
        pairs[i : i + slots, :] = mm(tok_ref[i : i + slots, :], wkv_ref[...]).astype(BF16)
    dreg[...] = jnp.zeros_like(dreg)
    qs[...] = mm(nest_ref[...], wq_ref[...]).astype(BF16)
    gs[...] = mm(dout_ref[...], wo_ref[...], 1, 1).astype(BF16)
    head_of = lax.broadcasted_iota(jnp.int32, (BT, feat), 1) // HD
    slot_row = lax.broadcasted_iota(jnp.int32, (slots, 2 * BT), 0)

    def block(b, carry):
        rows = pl.ds(pl.multiple_of(b * BT, BT), BT)
        live = len_ref[b] * GB
        for j in range(LIST):
            start = pl.multiple_of(lax.rem(ids_ref[b, j], SUB) * GB, GB)
            foot[j * GB : (j + 1) * GB, :] = pairs[pl.ds(start, GB), :]
        foot_t[...] = foot[...].T
        q = qs[rows, :]
        g = gs[rows, :]
        zero = jnp.zeros_like(q)
        for h in range(heads):
            qst[h * BT : (h + 1) * BT, :] = jnp.where(head_of == h, q, zero)
            gst[h * BT : (h + 1) * BT, :] = jnp.where(head_of == h, g, zero)
        att_parts = []
        dq_parts = []
        for hp in range(heads // 2):
            two = slice(hp * 2 * BT, (hp + 1) * 2 * BT)
            s = mm(foot[:, :feat], qst[two, :], 1, 1)
            dp = mm(foot[:, feat:], gst[two, :], 1, 1)
            s = jnp.where(slot_row < live, s, -jnp.inf)
            top = jnp.max(s, axis=0, keepdims=True)
            e = jnp.exp2((s - top) * (scale * math.log2(math.e)))
            p = e * (1.0 / jnp.sum(e, axis=0, keepdims=True))
            p_low = p.astype(BF16)
            pst[:, two] = p_low
            centre = jnp.sum(p * dp, axis=0, keepdims=True)
            d_s = (p * (dp - centre) * scale).astype(BF16)
            dst[:, two] = d_s
            cols = slice(hp * 2 * HD, (hp + 1) * 2 * HD)
            vals = slice(feat + hp * 2 * HD, feat + (hp + 1) * 2 * HD)
            a_t = mm(foot_t[vals, :], p_low)
            q_t = mm(foot_t[cols, :], d_s)
            att_parts += [a_t[:HD, :BT], a_t[HD:, BT:]]
            dq_parts += [q_t[:HD, :BT], q_t[HD:, BT:]]
        att[rows, :] = jnp.concatenate(att_parts, axis=0).T.astype(BF16)
        dq[rows, :] = jnp.concatenate(dq_parts, axis=0).T.astype(BF16)
        d_k = mm(dst[...], qst[...])
        d_v = mm(pst[...], gst[...])
        for j in range(LIST):
            start = pl.multiple_of(lax.rem(ids_ref[b, j], SUB) * GB, GB)
            part = slice(j * GB, (j + 1) * GB)
            dreg[pl.ds(start, GB), :feat] += d_k[part, :]
            dreg[pl.ds(start, GB), feat:] += d_v[part, :]
        return carry

    lax.fori_loop(0, nest_ref.shape[0] // BT, block, 0)
    out_ref[...] = mm(att[...], wo_ref[...]).astype(BF16)
    dnest_ref[...] = mm(dq[...], wq_ref[...], 1, 1).astype(BF16)
    w_rows = 2 * feat // SUB
    kv = jnp.zeros((feat, 2 * feat), F32)
    for i in range(0, SUB * GB, slots):
        part = dreg[i : i + slots, :]
        high = part.astype(BF16)
        low = (part - high.astype(F32)).astype(BF16)
        tok = tok_ref[i : i + slots, :]
        kv = kv + mm(tok, high, 0, 0) + mm(tok, low, 0, 0)
        for g in range(LIST):
            for n in range(2 * feat // CH):
                pay_ref[n, i // GB + g] = high[
                    g * GB : (g + 1) * GB, n * CH : (n + 1) * CH
                ]
    grad_q = mm(nest_ref[...], dq[...], 0, 0).astype(BF16)
    grad_o = mm(att[...], dout_ref[...], 0, 0).astype(BF16)
    kv = kv.astype(BF16)
    for k in range(SUB // 2):
        part = slice(k * w_rows, (k + 1) * w_rows)
        wpay_ref[0, k] = kv[part, :feat]
        wpay_ref[1, k] = kv[part, feat:]
        wpay_ref[0, SUB // 2 + k] = grad_q[part, :]
        wpay_ref[1, SUB // 2 + k] = grad_o[part, :]


CH = 128


def reduce_kernel(pay_ref, wpay_ref, wkv_ref, dglob_ref, wg, *rest):
    pair_bufs, weight_bufs, (own, send, recv) = rest[:8], rest[8:16], rest[16:]
    base, *at = coords()
    to = partners(base, *at)
    zh, zl, y, c = at
    feat = wkv_ref.shape[0]
    chunks = pay_ref.shape[0]
    greet(to)
    copy = sender(send, recv)

    def keep_pairs(k):
        def done(total):
            own[:, k * CH : (k + 1) * CH] = total

        return done

    def keep_weights(k):
        def done(total):
            wg[zh, zl, y, c, :, k * feat : (k + 1) * feat] = total.astype(BF16)

        return done

    steps = {}
    for k in range(2):
        bufs = [buf.at[k] for buf in weight_bufs]
        steps["w", k] = halve_steps(
            k == 0, wpay_ref.at[k], bufs, copy, 4 * k, at, to, keep_weights(k)
        )
    for k in range(chunks):
        bufs = [buf.at[k] for buf in pair_bufs]
        steps["p", k] = halve_steps(
            k < chunks // 2, pay_ref.at[k], bufs, copy, 8 + 4 * k, at, to, keep_pairs(k)
        )
    share = gather_steps(wg, wg.shape[4] // 2, copy, 8 + 4 * chunks, at, to)

    def weights():
        for k in range(2):
            next(steps["w", k])

    def pairs(first):
        for k in range(first, chunks // 2, 2):
            next(steps["p", k])
            next(steps["p", k + chunks // 2])

    weights()
    pairs(0)
    pairs(1)
    weights()
    pairs(0)
    weights()
    pairs(1)
    weights()
    pairs(0)
    weights()
    next(share)
    pairs(1)
    next(share)
    pairs(0)
    next(share)
    pairs(1)
    next(share)
    pairs(0)
    pairs(1)
    part = own[...]
    high = part.astype(BF16)
    low = (part - high.astype(F32)).astype(BF16)
    total = mm(high, wkv_ref[...], 1, 1) + mm(low, wkv_ref[...], 1, 1)
    dglob_ref[...] = total.astype(BF16)
    next(share)
    weights()
    pairs(0)
    pairs(1)


def finish_kernel(norm, dglob_in, wg_ref, dglob_ref, gq_ref, gkv_ref, go_ref):
    feat = gq_ref.shape[0]
    dglob_ref[...] = dglob_in[...]
    gkv_ref[...] = wg_ref[:feat, :].astype(F32) * norm
    gq_ref[...] = wg_ref[feat:, :feat].astype(F32) * norm
    go_ref[...] = wg_ref[feat:, feat:].astype(F32) * norm


def vmem(n):
    return [pl.BlockSpec(memory_space=pltpu.VMEM)] * n


def shards(nest_tokens, global_tokens, block_ids, list_length, w_query, w_keyval, w_out, d_output):
    rows, feat = nest_tokens.shape
    band = lax.axis_size("band")
    norm = 1.0 / math.sqrt(rows * band)
    tokens = pl.pallas_call(
        gather_kernel,
        out_shape=jax.ShapeDtypeStruct((2, 2, 2, 2, GB, feat), BF16),
        in_specs=vmem(1),
        out_specs=vmem(1)[0],
        scratch_shapes=[pltpu.SemaphoreType.DMA((4 * PIECES,))] * 2,
        compiler_params=pltpu.CompilerParams(
            collective_id=0, has_side_effects=True, vmem_limit_bytes=VMEM_LIMIT
        ),
    )(global_tokens)
    tokens = tokens.reshape(SUB * GB, feat)
    slots = LIST * GB
    wide = feat // HD * BT
    few = 2 * feat // SUB
    smem = [pl.BlockSpec(memory_space=pltpu.SMEM)] * 2
    output, d_nest, payload, wide_payload = pl.pallas_call(
        attend_kernel,
        out_shape=(
            jax.ShapeDtypeStruct((rows, feat), BF16),
            jax.ShapeDtypeStruct((rows, feat), BF16),
            jax.ShapeDtypeStruct((2 * feat // CH, SUB, GB, CH), BF16),
            jax.ShapeDtypeStruct((2, SUB, few, feat), BF16),
        ),
        in_specs=smem + vmem(6),
        out_specs=tuple(vmem(4)),
        scratch_shapes=[
            pltpu.VMEM((SUB * GB, 2 * feat), BF16),
            pltpu.VMEM((rows, feat), BF16),
            pltpu.VMEM((rows, feat), BF16),
            pltpu.VMEM((rows, feat), BF16),
            pltpu.VMEM((rows, feat), BF16),
            pltpu.VMEM((SUB * GB, 2 * feat), F32),
            pltpu.VMEM((slots, 2 * feat), BF16),
            pltpu.VMEM((2 * feat, slots), BF16),
            pltpu.VMEM((wide, feat), BF16),
            pltpu.VMEM((wide, feat), BF16),
            pltpu.VMEM((slots, wide), BF16),
            pltpu.VMEM((slots, wide), BF16),
        ],
        compiler_params=pltpu.CompilerParams(vmem_limit_bytes=VMEM_LIMIT),
    )(block_ids, list_length, tokens, nest_tokens, d_output, w_query, w_keyval, w_out)
    n = 2 * feat // CH
    payload = payload.reshape(n, 2, 2, 2, 2, GB, CH)
    wide_payload = wide_payload.reshape(2, 2, 2, 2, 2, few, feat)
    scratch = []
    for count, block in ((n, (GB, CH)), (2, (few, feat))):
        for lead, dtype in (
            ((2, 2, 2), BF16), ((2, 2), BF16), ((2, 2), BF16), ((2, 2), F32),
            ((2,), BF16), ((2,), BF16), ((), BF16), ((), BF16),
        ):
            scratch.append(pltpu.VMEM((count, *lead, *block), dtype))
    copies = 8 + 4 * n + 6
    d_global, sums = pl.pallas_call(
        reduce_kernel,
        out_shape=(
            jax.ShapeDtypeStruct((GB, feat), BF16),
            jax.ShapeDtypeStruct((2, 2, 2, 2, few, 2 * feat), BF16),
        ),
        in_specs=vmem(3),
        out_specs=tuple(vmem(2)),
        scratch_shapes=scratch + [
            pltpu.VMEM((GB, 2 * feat), F32),
            pltpu.SemaphoreType.DMA((copies,)),
            pltpu.SemaphoreType.DMA((copies,)),
        ],
        compiler_params=pltpu.CompilerParams(
            collective_id=1, has_side_effects=True, vmem_limit_bytes=VMEM_LIMIT
        ),
    )(payload, wide_payload, w_keyval)
    d_global, grad_q, grad_kv, grad_o = pl.pallas_call(
        functools.partial(finish_kernel, norm),
        out_shape=(
            jax.ShapeDtypeStruct((GB, feat), BF16),
            jax.ShapeDtypeStruct((feat, feat), F32),
            jax.ShapeDtypeStruct((feat, 2 * feat), F32),
            jax.ShapeDtypeStruct((feat, feat), F32),
        ),
        in_specs=vmem(2),
        out_specs=tuple(vmem(4)),
        compiler_params=pltpu.CompilerParams(vmem_limit_bytes=VMEM_LIMIT),
    )(d_global, sums.reshape(2 * feat, 2 * feat))
    if band > SUB:
        groups = [[s + SUB * k for k in range(band // SUB)] for s in range(SUB)]
        grad_q, grad_kv, grad_o = lax.psum(
            (grad_q, grad_kv, grad_o), "band", axis_index_groups=groups
        )
    return output, d_nest, d_global, grad_q, grad_kv, grad_o


def solution(mesh):
    both = ("groups", "band")
    in_specs = (
        P(both, None), P(both, None), P(both, None), P(both), P(), P(), P(), P(both, None),
    )
    out_specs = (
        P(both, None), P(both, None), P(both, None),
        P("groups", None), P("groups", None), P("groups", None),
    )
    return jax.shard_map(shards, mesh=mesh, in_specs=in_specs, out_specs=out_specs, check_vma=False)
```

```python
import functools
import math

import jax
import jax.numpy as jnp
from jax import lax
from jax.experimental import pallas as pl
from jax.experimental.pallas import tpu as pltpu
from jax.sharding import PartitionSpec as P

HD = 32
BT = 128
GB = 128
LIST = 4
SUB = 16
F32 = jnp.float32
BF16 = jnp.bfloat16
VMEM_LIMIT = 56 * 1024 * 1024


def mm(a, b, ca=1, cb=0):
    return lax.dot_general(a, b, (((ca,), (cb,)), ((), ())), preferred_element_type=F32)


def coords():
    me = lax.axis_index("band")
    pos = me % SUB
    return me - pos, pos // 8, pos // 4 % 2, pos // 2 % 2, pos % 2


def partners(base, zh, zl, y, c):
    def at(a, b, d, e):
        return {"band": base + a * 8 + b * 4 + d * 2 + e}

    far = at(1 - zh, zl, y, c)
    near = at(zh, 1 - zl, y, c)
    side = at(zh, zl, 1 - y, c)
    core = at(zh, zl, y, 1 - c)
    return far, near, side, core


def greet(devices):
    barrier = pltpu.get_barrier_semaphore()
    for device in devices:
        pl.semaphore_signal(barrier, inc=1, device_id=device, device_id_type=pl.DeviceIdType.MESH)
    pl.semaphore_wait(barrier, len(devices))


def sender(send, recv):
    def copy(src, dst, k, device):
        op = pltpu.make_async_remote_copy(
            src_ref=src,
            dst_ref=dst,
            send_sem=send.at[k],
            recv_sem=recv.at[k],
            device_id=device,
            device_id_type=pl.DeviceIdType.MESH,
        )
        op.start()
        return op

    return copy


def gather_steps(buf, half, copy, first, at, to):
    zh, zl, y, c = at
    far, near, side, core = to
    lo, hi = pl.ds(0, half), pl.ds(half, half)

    def go(ref, k, device):
        return copy(ref, ref, first + k, device)

    ops = [go(buf.at[zh, zl, y, c], 0, far)]
    yield
    ops[0].wait_recv()
    ops.append(go(buf.at[:, zl, y, c, lo], 1, side))
    ops.append(go(buf.at[:, zl, y, c, hi], 2, near))
    yield
    ops[1].wait_recv()
    ops.append(go(buf.at[:, zl, :, c, lo], 3, near))
    ops[2].wait_recv()
    ops.append(go(buf.at[:, :, y, c, hi], 4, side))
    yield
    ops[3].wait_recv()
    ops[4].wait_recv()
    ops.append(go(buf.at[:, :, :, c], 5, core))
    yield
    ops[5].wait_recv()
    for op in ops:
        op.wait_send()
    yield


def halve_steps(side_first, pay, bufs, copy, k, at, to, done):
    ra, s_buf, r_buf, kept, t_buf, u_buf, v_buf, x_buf = bufs
    zh, zl, y, c = at
    far, near, side, core = to
    ops = [copy(pay.at[:, :, :, 1 - c], ra, k, core)]
    yield
    ops[0].wait_recv()
    if side_first:
        sent = pay[:, :, 1 - y, c].astype(F32) + ra[:, :, 1 - y].astype(F32)
    else:
        sent = pay[:, 1 - zl, :, c].astype(F32) + ra[:, 1 - zl].astype(F32)
    s_buf[...] = sent.astype(BF16)
    ops.append(copy(s_buf, r_buf, k + 1, side if side_first else near))
    if side_first:
        kept[...] = pay[:, :, y, c].astype(F32) + ra[:, :, y].astype(F32)
    else:
        kept[...] = pay[:, zl, :, c].astype(F32) + ra[:, zl].astype(F32)
    mine = zl if side_first else y
    yield
    ops[1].wait_recv()
    t_buf[...] = (kept[:, 1 - mine] + r_buf[:, 1 - mine].astype(F32)).astype(BF16)
    ops.append(copy(t_buf, u_buf, k + 2, near if side_first else side))
    yield
    ops[2].wait_recv()
    v_buf[...] = (
        kept[1 - zh, mine] + r_buf[1 - zh, mine].astype(F32) + u_buf[1 - zh].astype(F32)
    ).astype(BF16)
    ops.append(copy(v_buf, x_buf, k + 3, far))
    yield
    ops[3].wait_recv()
    part = kept[zh, mine] + r_buf[zh, mine].astype(F32) + u_buf[zh].astype(F32)
    done(part + x_buf[...].astype(F32))
    yield
    for op in ops:
        op.wait_send()
    yield


def spread_steps(side_first, buf, rows, copy, k, at, to):
    zh, zl, y, c = at
    far, near, side, core = to

    def go(ref, device):
        ops.append(copy(ref, ref, k + len(ops), device))

    ops = []
    go(buf.at[zh, zl, y, c, rows], far)
    yield
    ops[0].wait_recv()
    go(buf.at[:, zl, y, c, rows], side if side_first else near)
    yield
    ops[1].wait_recv()
    if side_first:
        go(buf.at[:, zl, :, c, rows], near)
    else:
        go(buf.at[:, :, y, c, rows], side)
    yield
    ops[2].wait_recv()
    go(buf.at[:, :, :, c, rows], core)
    yield
    ops[3].wait_recv()
    for op in ops:
        op.wait_send()
    yield


PIECES = 4


def gather_kernel(tok_ref, all_ref, send, recv):
    base, *at = coords()
    to = partners(base, *at)
    zh, zl, y, c = at
    all_ref[zh, zl, y, c] = tok_ref[...]
    greet(to)
    copy = sender(send, recv)
    size = tok_ref.shape[0] // PIECES
    steps = [
        spread_steps(k % 2 == 0, all_ref, pl.ds(k * size, size), copy, 4 * k, at, to)
        for k in range(PIECES)
    ]
    for _ in range(5):
        for step in steps:
            next(step)


def attend_kernel(
    ids_ref, len_ref, tok_ref, nest_ref, dout_ref, wq_ref, wkv_ref, wo_ref,
    out_ref, dnest_ref, pay_ref, wpay_ref,
    pairs, qs, gs, att, dq, dreg, foot, foot_t, qst, gst, pst, dst,
):
    feat = nest_ref.shape[1]
    slots = LIST * GB
    heads = feat // HD
    scale = HD ** (-0.5)
    for i in range(0, SUB * GB, slots):
        pairs[i : i + slots, :] = mm(tok_ref[i : i + slots, :], wkv_ref[...]).astype(BF16)
    dreg[...] = jnp.zeros_like(dreg)
    qs[...] = mm(nest_ref[...], wq_ref[...]).astype(BF16)
    gs[...] = mm(dout_ref[...], wo_ref[...], 1, 1).astype(BF16)
    head_of = lax.broadcasted_iota(jnp.int32, (BT, feat), 1) // HD
    slot_row = lax.broadcasted_iota(jnp.int32, (slots, 2 * BT), 0)

    def block(b, carry):
        rows = pl.ds(pl.multiple_of(b * BT, BT), BT)
        live = len_ref[b] * GB
        for j in range(LIST):
            start = pl.multiple_of(lax.rem(ids_ref[b, j], SUB) * GB, GB)
            foot[j * GB : (j + 1) * GB, :] = pairs[pl.ds(start, GB), :]
        foot_t[...] = foot[...].T
        q = qs[rows, :]
        g = gs[rows, :]
        zero = jnp.zeros_like(q)
        for h in range(heads):
            qst[h * BT : (h + 1) * BT, :] = jnp.where(head_of == h, q, zero)
            gst[h * BT : (h + 1) * BT, :] = jnp.where(head_of == h, g, zero)
        att_parts = []
        dq_parts = []
        for hp in range(heads // 2):
            two = slice(hp * 2 * BT, (hp + 1) * 2 * BT)
            s = mm(foot[:, :feat], qst[two, :], 1, 1)
            dp = mm(foot[:, feat:], gst[two, :], 1, 1)
            s = jnp.where(slot_row < live, s, -jnp.inf)
            top = jnp.max(s, axis=0, keepdims=True)
            e = jnp.exp2((s - top) * (scale * math.log2(math.e)))
            p = e * (1.0 / jnp.sum(e, axis=0, keepdims=True))
            p_low = p.astype(BF16)
            pst[:, two] = p_low
            centre = jnp.sum(p * dp, axis=0, keepdims=True)
            d_s = (p * (dp - centre) * scale).astype(BF16)
            dst[:, two] = d_s
            cols = slice(hp * 2 * HD, (hp + 1) * 2 * HD)
            vals = slice(feat + hp * 2 * HD, feat + (hp + 1) * 2 * HD)
            a_t = mm(foot_t[vals, :], p_low)
            q_t = mm(foot_t[cols, :], d_s)
            att_parts += [a_t[:HD, :BT], a_t[HD:, BT:]]
            dq_parts += [q_t[:HD, :BT], q_t[HD:, BT:]]
        att[rows, :] = jnp.concatenate(att_parts, axis=0).T.astype(BF16)
        dq[rows, :] = jnp.concatenate(dq_parts, axis=0).T.astype(BF16)
        d_k = mm(dst[...], qst[...])
        d_v = mm(pst[...], gst[...])
        for j in range(LIST):
            start = pl.multiple_of(lax.rem(ids_ref[b, j], SUB) * GB, GB)
            part = slice(j * GB, (j + 1) * GB)
            dreg[pl.ds(start, GB), :feat] += d_k[part, :]
            dreg[pl.ds(start, GB), feat:] += d_v[part, :]
        return carry

    lax.fori_loop(0, nest_ref.shape[0] // BT, block, 0)
    out_ref[...] = mm(att[...], wo_ref[...]).astype(BF16)
    dnest_ref[...] = mm(dq[...], wq_ref[...], 1, 1).astype(BF16)
    w_rows = 2 * feat // SUB
    kv = jnp.zeros((feat, 2 * feat), F32)
    for i in range(0, SUB * GB, slots):
        part = dreg[i : i + slots, :]
        high = part.astype(BF16)
        low = (part - high.astype(F32)).astype(BF16)
        tok = tok_ref[i : i + slots, :]
        kv = kv + mm(tok, high, 0, 0) + mm(tok, low, 0, 0)
        for g in range(LIST):
            for n in range(2 * feat // CH):
                pay_ref[n, i // GB + g] = high[
                    g * GB : (g + 1) * GB, n * CH : (n + 1) * CH
                ]
    grad_q = mm(nest_ref[...], dq[...], 0, 0).astype(BF16)
    grad_o = mm(att[...], dout_ref[...], 0, 0).astype(BF16)
    kv = kv.astype(BF16)
    for k in range(SUB // 2):
        part = slice(k * w_rows, (k + 1) * w_rows)
        wpay_ref[0, k] = kv[part, :feat]
        wpay_ref[1, k] = kv[part, feat:]
        wpay_ref[0, SUB // 2 + k] = grad_q[part, :]
        wpay_ref[1, SUB // 2 + k] = grad_o[part, :]


CH = 128


def reduce_kernel(pay_ref, wpay_ref, wkv_ref, dglob_ref, wg, *rest):
    pair_bufs, weight_bufs, (own, send, recv) = rest[:8], rest[8:16], rest[16:]
    base, *at = coords()
    to = partners(base, *at)
    zh, zl, y, c = at
    feat = wkv_ref.shape[0]
    chunks = pay_ref.shape[0]
    greet(to)
    copy = sender(send, recv)

    def keep_pairs(k):
        def done(total):
            own[:, k * CH : (k + 1) * CH] = total

        return done

    def keep_weights(k):
        def done(total):
            wg[zh, zl, y, c, :, k * feat : (k + 1) * feat] = total.astype(BF16)

        return done

    steps = {}
    for k in range(2):
        bufs = [buf.at[k] for buf in weight_bufs]
        steps["w", k] = halve_steps(
            k == 0, wpay_ref.at[k], bufs, copy, 4 * k, at, to, keep_weights(k)
        )
    for k in range(chunks):
        bufs = [buf.at[k] for buf in pair_bufs]
        steps["p", k] = halve_steps(
            k < chunks // 2, pay_ref.at[k], bufs, copy, 8 + 4 * k, at, to, keep_pairs(k)
        )
    share = gather_steps(wg, wg.shape[4] // 2, copy, 8 + 4 * chunks, at, to)

    def weights():
        for k in range(2):
            next(steps["w", k])

    def pairs(first):
        for k in range(first, chunks // 2, 2):
            next(steps["p", k])
            next(steps["p", k + chunks // 2])

    weights()
    pairs(0)
    pairs(1)
    weights()
    pairs(0)
    weights()
    pairs(1)
    weights()
    pairs(0)
    weights()
    next(share)
    pairs(1)
    next(share)
    pairs(0)
    next(share)
    pairs(1)
    next(share)
    pairs(0)
    pairs(1)
    part = own[...]
    high = part.astype(BF16)
    low = (part - high.astype(F32)).astype(BF16)
    total = mm(high, wkv_ref[...], 1, 1) + mm(low, wkv_ref[...], 1, 1)
    dglob_ref[...] = total.astype(BF16)
    next(share)
    weights()
    pairs(0)
    pairs(1)


def finish_kernel(norm, dglob_in, wg_ref, dglob_ref, gq_ref, gkv_ref, go_ref):
    feat = gq_ref.shape[0]
    dglob_ref[...] = dglob_in[...]
    gkv_ref[...] = wg_ref[:feat, :].astype(F32) * norm
    gq_ref[...] = wg_ref[feat:, :feat].astype(F32) * norm
    go_ref[...] = wg_ref[feat:, feat:].astype(F32) * norm


def vmem(n):
    return [pl.BlockSpec(memory_space=pltpu.VMEM)] * n


def shards(nest_tokens, global_tokens, block_ids, list_length, w_query, w_keyval, w_out, d_output):
    rows, feat = nest_tokens.shape
    band = lax.axis_size("band")
    norm = 1.0 / math.sqrt(rows * band)
    tokens = pl.pallas_call(
        gather_kernel,
        out_shape=jax.ShapeDtypeStruct((2, 2, 2, 2, GB, feat), BF16),
        in_specs=vmem(1),
        out_specs=vmem(1)[0],
        scratch_shapes=[pltpu.SemaphoreType.DMA((4 * PIECES,))] * 2,
        compiler_params=pltpu.CompilerParams(
            collective_id=0, has_side_effects=True, vmem_limit_bytes=VMEM_LIMIT
        ),
    )(global_tokens)
    tokens = tokens.reshape(SUB * GB, feat)
    slots = LIST * GB
    wide = feat // HD * BT
    few = 2 * feat // SUB
    smem = [pl.BlockSpec(memory_space=pltpu.SMEM)] * 2
    output, d_nest, payload, wide_payload = pl.pallas_call(
        attend_kernel,
        out_shape=(
            jax.ShapeDtypeStruct((rows, feat), BF16),
            jax.ShapeDtypeStruct((rows, feat), BF16),
            jax.ShapeDtypeStruct((2 * feat // CH, SUB, GB, CH), BF16),
            jax.ShapeDtypeStruct((2, SUB, few, feat), BF16),
        ),
        in_specs=smem + vmem(6),
        out_specs=tuple(vmem(4)),
        scratch_shapes=[
            pltpu.VMEM((SUB * GB, 2 * feat), BF16),
            pltpu.VMEM((rows, feat), BF16),
            pltpu.VMEM((rows, feat), BF16),
            pltpu.VMEM((rows, feat), BF16),
            pltpu.VMEM((rows, feat), BF16),
            pltpu.VMEM((SUB * GB, 2 * feat), F32),
            pltpu.VMEM((slots, 2 * feat), BF16),
            pltpu.VMEM((2 * feat, slots), BF16),
            pltpu.VMEM((wide, feat), BF16),
            pltpu.VMEM((wide, feat), BF16),
            pltpu.VMEM((slots, wide), BF16),
            pltpu.VMEM((slots, wide), BF16),
        ],
        compiler_params=pltpu.CompilerParams(vmem_limit_bytes=VMEM_LIMIT),
    )(block_ids, list_length, tokens, nest_tokens, d_output, w_query, w_keyval, w_out)
    n = 2 * feat // CH
    payload = payload.reshape(n, 2, 2, 2, 2, GB, CH)
    wide_payload = wide_payload.reshape(2, 2, 2, 2, 2, few, feat)
    scratch = []
    for count, block in ((n, (GB, CH)), (2, (few, feat))):
        for lead, dtype in (
            ((2, 2, 2), BF16), ((2, 2), BF16), ((2, 2), BF16), ((2, 2), F32),
            ((2,), BF16), ((2,), BF16), ((), BF16), ((), BF16),
        ):
            scratch.append(pltpu.VMEM((count, *lead, *block), dtype))
    copies = 8 + 4 * n + 6
    d_global, sums = pl.pallas_call(
        reduce_kernel,
        out_shape=(
            jax.ShapeDtypeStruct((GB, feat), BF16),
            jax.ShapeDtypeStruct((2, 2, 2, 2, few, 2 * feat), BF16),
        ),
        in_specs=vmem(3),
        out_specs=tuple(vmem(2)),
        scratch_shapes=scratch + [
            pltpu.VMEM((GB, 2 * feat), F32),
            pltpu.SemaphoreType.DMA((copies,)),
            pltpu.SemaphoreType.DMA((copies,)),
        ],
        compiler_params=pltpu.CompilerParams(
            collective_id=1, has_side_effects=True, vmem_limit_bytes=VMEM_LIMIT
        ),
    )(payload, wide_payload, w_keyval)
    d_global, grad_q, grad_kv, grad_o = pl.pallas_call(
        functools.partial(finish_kernel, norm),
        out_shape=(
            jax.ShapeDtypeStruct((GB, feat), BF16),
            jax.ShapeDtypeStruct((feat, feat), F32),
            jax.ShapeDtypeStruct((feat, 2 * feat), F32),
            jax.ShapeDtypeStruct((feat, feat), F32),
        ),
        in_specs=vmem(2),
        out_specs=tuple(vmem(4)),
        compiler_params=pltpu.CompilerParams(vmem_limit_bytes=VMEM_LIMIT),
    )(d_global, sums.reshape(2 * feat, 2 * feat))
    if band > SUB:
        groups = [[s + SUB * k for k in range(band // SUB)] for s in range(SUB)]
        grad_q, grad_kv, grad_o = lax.psum(
            (grad_q, grad_kv, grad_o), "band", axis_index_groups=groups
        )
    return output, d_nest, d_global, grad_q, grad_kv, grad_o


def solution(mesh):
    both = ("groups", "band")
    in_specs = (
        P(both, None), P(both, None), P(both, None), P(both), P(), P(), P(), P(both, None),
    )
    out_specs = (
        P(both, None), P(both, None), P(both, None),
        P("groups", None), P("groups", None), P("groups", None),
    )
    return jax.shard_map(shards, mesh=mesh, in_specs=in_specs, out_specs=out_specs, check_vma=False)
```
